32 devices in a mesh: groups: 2 (over y), dev: 4 (over z), sub: 4 (over x, core).
Axes of the slice: x: 2, y: 2, z: 4, core: 2. Of those that a mesh axis runs over, the one named last changes fastest.
Arguments:
- embeds: float32 [4096, 1024], P(('groups', 'dev', 'sub')), parts along dimension 0
- assignment: int32 [4096], P(('groups', 'dev', 'sub')), parts along dimension 0, may hold values from 0 to 15, as said below
Outputs:
- best_match: float32 [4096], P(('groups', 'dev', 'sub')), parts along dimension 0
The draws below stay inside these ranges and needn't reach their ends.
There are 2 independent parts, one for each index of `groups`. The reference program is written for one: setup_inputs(seed, part) draws one part's arguments, and reference() takes and returns one part's arrays. A program takes and returns all parts, laid end to end along the dimension named above; each array names one. Nothing has to cross between parts.
Inputs may be any that keep to these rules, and one draw needn't show every extreme that they name: `assignment`: cluster c is owned by index c // 4 of sub. Among the points of one device, at most 64 have clusters owned by one index of sub, and exactly that many in every device.
All inputs are finite; a program needn't handle non-finite values.
Results may differ from the reference program's by a relative error of at most 0.0003.
Values may be sent and summed in bfloat16 or wider, within the bound.
No kernel may reach another device: no remote copies, remote signals or barrier semaphores. Data moves between devices by JAX's collectives and lax.ppermute only.
A program may use at most 64 MiB of HBM per device.

```python
import math
import jax
import jax.numpy as jnp
from jax import lax

E = 1024
ROWS_DEV = 128
K_SUB = 4
NPTS = 2048
CLUSTERS = 16
DUPS = 64


def layout_clusters(key):
    key = jax.random.fold_in(key, 11)
    key_star, key_other, key_order, key_pick = jax.random.split(key, 4)
    blocks = NPTS // ROWS_DEV
    owners = CLUSTERS // K_SUB
    capacity = ROWS_DEV // 2
    star = jax.random.randint(key_star, (blocks, 1), 0, owners)
    other = jax.random.randint(key_other, (blocks, ROWS_DEV - capacity), 0, owners - 1)
    other = (star + 1 + other) % owners
    pattern = jnp.concatenate([jnp.broadcast_to(star, (blocks, capacity)), other], axis=1)
    orders = jax.vmap(lambda sub_key: jax.random.permutation(sub_key, ROWS_DEV))(jax.random.split(key_order, blocks))
    target = jnp.take_along_axis(pattern, orders, axis=1)
    pick = jax.random.randint(key_pick, (blocks, ROWS_DEV), 0, K_SUB)
    return (target * K_SUB + pick).reshape(NPTS).astype(jnp.int32)


def draw_assignment(key, part):
    return layout_clusters(key)


def draw_embeds(key, part):
    clusters = layout_clusters(key)
    key = jax.random.fold_in(key, 5)
    key_dup, key_group, key_center, key_noise, key_weight = jax.random.split(key, 5)
    dup_index = jax.random.randint(key_dup, (NPTS,), 0, DUPS)
    group_ids = clusters * DUPS + dup_index
    shared = jax.vmap(lambda ident: jax.random.normal(jax.random.fold_in(key_group, ident), (E,), jnp.float32))(group_ids)
    centers = jax.vmap(lambda ident: jax.random.normal(jax.random.fold_in(key_center, ident), (E,), jnp.float32))(clusters)
    weights = jnp.exp(jax.random.uniform(key_weight, (NPTS, 1), jnp.float32, jnp.log(0.5), jnp.log(3.0)))
    noise = jax.random.normal(key_noise, (NPTS, E), jnp.float32)
    mixed = 0.7 * centers + noise + weights * shared
    return (mixed / jnp.sqrt(jnp.float32(E))).astype(jnp.float32)


def setup_inputs(seed: int = 0, part: int = 0) -> dict:
    splits = jax.random.split(jax.random.key(seed), 3)
    part_keys = jax.random.split(jax.random.fold_in(splits[2], part), 3)
    embeds = draw_embeds(jax.random.fold_in(jax.random.fold_in(splits[2], part), 71), part)
    assignment = draw_assignment(jax.random.fold_in(jax.random.fold_in(splits[2], part), 71), part)
    return dict(embeds=embeds, assignment=assignment)


def reference(embeds, assignment):
    squares = lax.optimization_barrier(jnp.sum(embeds * embeds, axis=1, keepdims=True))
    unit_rows = (embeds * lax.rsqrt(squares + 1e-06)).astype(jnp.bfloat16).astype(jnp.float32)
    total = unit_rows.shape[0]
    block_rows = math.gcd(total, 512)
    columns = jnp.arange(total, dtype=jnp.int32)

    def one_block(block_index):
        start = block_index * block_rows
        rows_here = lax.dynamic_slice_in_dim(unit_rows, start, block_rows, 0)
        ids_here = lax.dynamic_slice_in_dim(assignment, start, block_rows, 0)
        scores = jnp.dot(rows_here, unit_rows.T, precision=lax.Precision.HIGHEST, preferred_element_type=jnp.float32)
        own_index = start + jnp.arange(block_rows, dtype=jnp.int32)
        same_group = (ids_here[:, None] == assignment[None, :]) & (own_index[:, None] != columns[None, :])
        masked = jnp.where(same_group, scores, jnp.float32(-1.0))
        return jnp.maximum(lax.optimization_barrier(jnp.max(masked, axis=1)), jnp.float32(-1.0))
    result = lax.map(one_block, jnp.arange(total // block_rows, dtype=jnp.int32))
    return result.reshape(total)
```

```python
import functools

import jax
import jax.numpy as jnp
from jax import lax
from jax.experimental import pallas as pl
from jax.experimental.pallas import tpu as pltpu
from jax.sharding import PartitionSpec as P

LANES = 128
ID_ROWS = 16
LOWEST = -1.0


def pack_kernel(embeds_ref, ids_ref, out_ref):
    rows, width = embeds_ref.shape
    embeds = embeds_ref[...]
    squares = jnp.sum(embeds * embeds, axis=1, keepdims=True)
    unit = (embeds * lax.rsqrt(squares + 1e-06)).astype(jnp.bfloat16)
    for block in range(width // LANES):
        out_ref[pl.ds(block * rows, rows), :] = unit[:, block * LANES : (block + 1) * LANES]
    ids = ids_ref[...].astype(jnp.float32)
    out_ref[pl.ds(width // LANES * rows, ID_ROWS), :] = jnp.broadcast_to(
        ids, (ID_ROWS, rows)
    ).astype(jnp.bfloat16)


def load_rows(ref, rows):
    blocks = (ref.shape[0] - ID_ROWS) // rows
    return jnp.concatenate([ref[pl.ds(b * rows, rows), :] for b in range(blocks)], axis=1)


def load_ids(ref, rows):
    start = ref.shape[0] - ID_ROWS
    return ref[pl.ds(start, ID_ROWS), :].astype(jnp.float32)[:1, :]


def row_maxima(masked):
    best = functools.reduce(jnp.maximum, masked)
    return jnp.max(best.T, axis=0, keepdims=True)


def score_kernel(*refs, rows, own, want_rows, want_columns):
    outs = int(want_rows) + int(want_columns)
    left_ref, column_refs, out_refs = refs[0], refs[1 : len(refs) - outs], refs[len(refs) - outs :]
    left = load_rows(left_ref, rows)
    left_ids = jnp.broadcast_to(load_ids(left_ref, rows), (rows, rows)).T
    masked = []
    for k, ref in enumerate(column_refs):
        scores = lax.dot_general(
            left,
            load_rows(ref, rows),
            (((1,), (1,)), ((), ())),
            preferred_element_type=jnp.float32,
        )
        same = left_ids == load_ids(ref, rows)
        if own and k == 0:
            down = lax.broadcasted_iota(jnp.int32, (rows, rows), 0)
            across = lax.broadcasted_iota(jnp.int32, (rows, rows), 1)
            same = same & (down != across)
        masked.append(jnp.where(same, scores, jnp.float32(LOWEST)))
    if want_rows:
        out_refs[0][...] = row_maxima(masked)
    if want_columns:
        for k, block in enumerate(masked):
            out_refs[-1][pl.ds(k, 1), :] = jnp.max(block, axis=0, keepdims=True)


def scores(left, column, rows, own=False, want_rows=True, want_columns=True):
    width = (left.shape[0] - ID_ROWS) // rows * LANES
    shapes = [(1, rows)] * want_rows + [(len(column), rows)] * want_columns
    return pl.pallas_call(
        functools.partial(
            score_kernel, rows=rows, own=own, want_rows=want_rows, want_columns=want_columns
        ),
        out_shape=[jax.ShapeDtypeStruct(shape, jnp.float32) for shape in shapes],
        cost_estimate=pl.CostEstimate(
            flops=2 * rows * rows * len(column) * width,
            bytes_accessed=2 * left.size * (1 + len(column)),
            transcendentals=0,
        ),
        compiler_params=pltpu.CompilerParams(vmem_limit_bytes=32 * 1024 * 1024),
    )(left, *column)


def pack(embeds, ids):
    rows, width = embeds.shape
    return pl.pallas_call(
        pack_kernel,
        out_shape=jax.ShapeDtypeStruct((width // LANES * rows + ID_ROWS, LANES), jnp.bfloat16),
        compiler_params=pltpu.CompilerParams(vmem_limit_bytes=32 * 1024 * 1024),
    )(embeds, ids.reshape(1, rows))


def column_order(count):
    return [0, 3, 1, 2] if count == 4 else list(range(count))


def on_device(embeds, assignment):
    rows = embeds.shape[0]
    columns, lanes = lax.axis_size("dev"), lax.axis_size("sub")
    order = column_order(columns)

    def along_dev(value, step):
        pairs = [(order[i], order[(i + step) % columns]) for i in range(columns)]
        return lax.ppermute(value, "dev", pairs)

    def along_sub(value, flip):
        return lax.ppermute(value, "sub", [(i, i ^ flip) for i in range(lanes)])

    own = pack(embeds, assignment)
    turns = list(range(1, (columns + 1) // 2))
    moved = {step: along_dev(own, step) for step in turns}
    swap = columns // 2 if columns % 2 == 0 else 0
    if swap:
        swapped = along_dev(own, swap)
    column = {0: own}
    for flip in range(2, lanes, 2):
        column[flip] = along_sub(own, flip)
    for flip in range(0, lanes, 2):
        column[flip + 1] = along_sub(column[flip], 1)
    column = [column[k] for k in range(lanes)]

    best = [scores(own, column, rows, own=True, want_columns=False)[0]]
    partial = []
    if swap:
        partial.append(scores(swapped, column, rows, want_rows=False)[0])
    for step in turns:
        row_best, column_best = scores(moved[step], column, rows)
        best.append(along_dev(row_best, -step))
        partial.append(column_best)
    total = functools.reduce(jnp.maximum, partial)
    pair = total[:2]
    for flip in range(2, lanes, 2):
        pair = jnp.maximum(pair, along_sub(total[flip : flip + 2], flip))
    best.append(pair[:1])
    best.append(along_sub(pair[1:], 1))
    return functools.reduce(jnp.maximum, best).reshape(rows)


def solution(mesh):
    placed = (P(("groups", "dev", "sub"), None), P(("groups", "dev", "sub")))
    return jax.shard_map(
        on_device,
        mesh=mesh,
        in_specs=placed,
        out_specs=P(("groups", "dev", "sub")),
        check_vma=False,
    )
```

```python
import functools

import jax
import jax.numpy as jnp
from jax import lax
from jax.experimental import pallas as pl
from jax.experimental.pallas import tpu as pltpu
from jax.sharding import PartitionSpec as P

LANES = 128
ID_ROWS = 16
LOWEST = -1.0
VMEM_BYTES = 16 * 1024 * 1024


def pack_kernel(embeds_ref, out_ref):
    rows, width = embeds_ref.shape
    embeds = embeds_ref[...]
    squares = jnp.sum(embeds * embeds, axis=1, keepdims=True)
    unit = (embeds * lax.rsqrt(squares + 1e-06)).astype(jnp.bfloat16)
    for block in range(width // LANES):
        out_ref[pl.ds(block * rows, rows), :] = unit[:, block * LANES : (block + 1) * LANES]


def label_kernel(packed_ref, ids_ref, out_ref):
    del packed_ref
    start = out_ref.shape[0] - ID_ROWS
    ids = jnp.broadcast_to(ids_ref[...].astype(jnp.float32), (ID_ROWS, ids_ref.shape[1]))
    out_ref[pl.ds(start, ID_ROWS), :] = ids.astype(jnp.bfloat16)


def pack(embeds, ids):
    rows, width = embeds.shape
    cells = width // LANES * rows
    shape = jax.ShapeDtypeStruct((cells + ID_ROWS, LANES), jnp.bfloat16)
    packed = pl.pallas_call(
        pack_kernel,
        out_shape=shape,
        compiler_params=pltpu.CompilerParams(vmem_limit_bytes=VMEM_BYTES),
    )(embeds)
    return pl.pallas_call(
        label_kernel,
        out_shape=shape,
        input_output_aliases={0: 0},
        compiler_params=pltpu.CompilerParams(vmem_limit_bytes=VMEM_BYTES),
    )(packed, ids.reshape(1, rows))


def load_rows(ref, rows):
    blocks = (ref.shape[0] - ID_ROWS) // rows
    return jnp.concatenate([ref[pl.ds(b * rows, rows), :] for b in range(blocks)], axis=1)


def load_ids(ref):
    start = ref.shape[0] - ID_ROWS
    return ref[pl.ds(start, ID_ROWS), :].astype(jnp.float32)[:1, :]


def masked_scores(left_refs, column_refs, rows, own):
    left = jnp.concatenate([load_rows(ref, rows) for ref in left_refs], axis=0)
    left_ids = [jnp.broadcast_to(load_ids(ref), (rows, rows)).T for ref in left_refs]
    masked = [[] for _ in left_refs]
    for k, ref in enumerate(column_refs):
        scores = lax.dot_general(
            left,
            load_rows(ref, rows),
            (((1,), (1,)), ((), ())),
            preferred_element_type=jnp.float32,
        )
        ids = load_ids(ref)
        for t in range(len(left_refs)):
            same = left_ids[t] == ids
            if own and k == 0:
                down = lax.broadcasted_iota(jnp.int32, (rows, rows), 0)
                across = lax.broadcasted_iota(jnp.int32, (rows, rows), 1)
                same = same & (down != across)
            part = scores[t * rows : (t + 1) * rows, :]
            masked[t].append(jnp.where(same, part, jnp.float32(LOWEST)))
    return masked


def row_maxima(masked):
    best = functools.reduce(jnp.maximum, masked)
    return jnp.max(best.T, axis=0, keepdims=True)


def own_kernel(*refs, rows):
    column, out_ref = refs[:-1], refs[-1]
    out_ref[...] = row_maxima(masked_scores(column[:1], column, rows, True)[0])


def moved_kernel(*refs, rows, turns, lefts):
    column, left, (turn_ref, part_ref) = refs[: -2 - lefts][::-1], refs[-2 - lefts : -2][::-1], refs[-2:]
    masked = masked_scores(left, column, rows, False)
    for t in range(turns):
        turn_ref[t] = row_maxima(masked[t])
    for k in range(len(column)):
        part = functools.reduce(jnp.maximum, [masked[t][k] for t in range(lefts)])
        part_ref[pl.ds(k, 1), :] = jnp.max(part, axis=0, keepdims=True)


def cost(lefts, column):
    cells = column[0].size
    return pl.CostEstimate(
        flops=2 * LANES * lefts * len(column) * cells,
        bytes_accessed=2 * cells * (lefts + len(column)),
        transcendentals=0,
    )


def column_order(count):
    return [0, 2, 1, 3] if count == 4 else list(range(count))


def on_device(embeds, assignment):
    rows = embeds.shape[0]
    columns, lanes = lax.axis_size("dev"), lax.axis_size("sub")
    order = column_order(columns)

    def along_dev(value, step):
        pairs = [(order[i], order[(i + step) % columns]) for i in range(columns)]
        return lax.ppermute(value, "dev", pairs)

    def along_sub(value, flip):
        return lax.ppermute(value, "sub", [(i, i ^ flip) for i in range(lanes)])

    own = pack(embeds, assignment)
    turns = list(range(1, (columns + 1) // 2))
    left = [along_dev(own, step) for step in turns]
    if columns % 2 == 0:
        left.append(along_dev(own, columns // 2))
    column = {0: own}
    for flip in range(2, lanes, 2):
        column[flip] = along_sub(own, flip)
    for flip in range(0, lanes, 2):
        column[flip + 1] = along_sub(column[flip], 1)
    column = [column[k] for k in range(lanes)]

    turn_best, part = pl.pallas_call(
        functools.partial(moved_kernel, rows=rows, turns=len(turns), lefts=len(left)),
        out_shape=[
            jax.ShapeDtypeStruct((len(turns), 1, rows), jnp.float32),
            jax.ShapeDtypeStruct((lanes, rows), jnp.float32),
        ],
        cost_estimate=cost(len(left), column),
        compiler_params=pltpu.CompilerParams(vmem_limit_bytes=VMEM_BYTES),
    )(*column[::-1], *left[::-1])
    own_best = pl.pallas_call(
        functools.partial(own_kernel, rows=rows),
        out_shape=jax.ShapeDtypeStruct((1, rows), jnp.float32),
        cost_estimate=cost(1, column),
        compiler_params=pltpu.CompilerParams(vmem_limit_bytes=VMEM_BYTES),
    )(*column)

    best = [own_best] + [along_dev(turn_best[t], -step) for t, step in enumerate(turns)]
    pair = part[:2]
    for flip in range(2, lanes, 2):
        pair = jnp.maximum(pair, along_sub(part[flip : flip + 2], flip))
    best.append(pair[:1])
    best.append(along_sub(pair[1:], 1))
    return functools.reduce(jnp.maximum, best).reshape(rows)


def solution(mesh):
    placed = (P(("groups", "dev", "sub"), None), P(("groups", "dev", "sub")))
    return jax.shard_map(
        on_device,
        mesh=mesh,
        in_specs=placed,
        out_specs=P(("groups", "dev", "sub")),
        check_vma=False,
    )
```

```python
import functools

import jax
import jax.numpy as jnp
from jax import lax
from jax.experimental import pallas as pl
from jax.experimental.pallas import tpu as pltpu
from jax.sharding import PartitionSpec as P

LANES = 128
ID_ROWS = 16
LOWEST = -1.0
CHUNKS = 1
VMEM_BYTES = 16 * 1024 * 1024


def pack_kernel(embeds_hbm, ids_hbm, out_ref, embeds_ref, ids_ref, embeds_sems, ids_sem):
    rows, width = embeds_ref.shape
    some = rows // CHUNKS
    copies = [
        pltpu.make_async_copy(
            embeds_hbm.at[pl.ds(c * some, some), :],
            embeds_ref.at[pl.ds(c * some, some), :],
            embeds_sems.at[c],
        )
        for c in range(CHUNKS)
    ]
    copy_ids = pltpu.make_async_copy(ids_hbm, ids_ref, ids_sem)
    copy_ids.start()
    for copy in copies:
        copy.start()
    copy_ids.wait()
    ids = ids_ref[...].astype(jnp.float32)
    out_ref[pl.ds(width // LANES * rows, ID_ROWS), :] = jnp.broadcast_to(
        ids, (ID_ROWS, rows)
    ).astype(jnp.bfloat16)
    for c, copy in enumerate(copies):
        copy.wait()
        embeds = embeds_ref[pl.ds(c * some, some), :]
        squares = jnp.sum(embeds * embeds, axis=1, keepdims=True)
        unit = (embeds * lax.rsqrt(squares + 1e-06)).astype(jnp.bfloat16)
        for block in range(width // LANES):
            out_ref[pl.ds(block * rows + c * some, some), :] = unit[
                :, block * LANES : (block + 1) * LANES
            ]


def pack(embeds, ids):
    rows, width = embeds.shape
    operands = [
        pltpu.with_memory_space_constraint(value, pltpu.HBM)
        for value in (embeds, ids.reshape(1, rows))
    ]
    return pl.pallas_call(
        pack_kernel,
        out_shape=jax.ShapeDtypeStruct((width // LANES * rows + ID_ROWS, LANES), jnp.bfloat16),
        in_specs=[pl.BlockSpec(memory_space=pltpu.HBM)] * 2,
        scratch_shapes=[
            pltpu.VMEM((rows, width), jnp.float32),
            pltpu.VMEM((1, rows), jnp.int32),
            pltpu.SemaphoreType.DMA((CHUNKS,)),
            pltpu.SemaphoreType.DMA,
        ],
        compiler_params=pltpu.CompilerParams(vmem_limit_bytes=VMEM_BYTES),
    )(*operands)


def load_rows(ref, rows):
    blocks = (ref.shape[0] - ID_ROWS) // rows
    return jnp.concatenate([ref[pl.ds(b * rows, rows), :] for b in range(blocks)], axis=1)


def load_ids(ref):
    start = ref.shape[0] - ID_ROWS
    return ref[pl.ds(start, ID_ROWS), :].astype(jnp.float32)[:1, :]


def masked_scores(left_refs, column_refs, rows, own):
    left = jnp.concatenate([load_rows(ref, rows) for ref in left_refs], axis=0)
    left_ids = [jnp.broadcast_to(load_ids(ref), (rows, rows)).T for ref in left_refs]
    masked = [[] for _ in left_refs]
    for k, ref in enumerate(column_refs):
        scores = lax.dot_general(
            left,
            load_rows(ref, rows),
            (((1,), (1,)), ((), ())),
            preferred_element_type=jnp.float32,
        )
        ids = load_ids(ref)
        for t in range(len(left_refs)):
            same = left_ids[t] == ids
            if own and k == 0:
                down = lax.broadcasted_iota(jnp.int32, (rows, rows), 0)
                across = lax.broadcasted_iota(jnp.int32, (rows, rows), 1)
                same = same & (down != across)
            part = scores[t * rows : (t + 1) * rows, :]
            masked[t].append(jnp.where(same, part, jnp.float32(LOWEST)))
    return masked


def row_maxima(masked):
    best = functools.reduce(jnp.maximum, masked)
    return jnp.max(best.T, axis=0, keepdims=True)


def own_kernel(*refs, rows, place):
    column = [refs[i] for i in place["column"]]
    refs[-1][...] = row_maxima(masked_scores(column[:1], column, rows, True)[0])


def moved_kernel(*refs, rows, place):
    left = [refs[i] for i in place["left"]]
    column = [refs[i] for i in place["column"]]
    turn_ref, part_ref = refs[-2:]
    masked = masked_scores(left, column, rows, False)
    for t in range(turn_ref.shape[0]):
        turn_ref[t] = row_maxima(masked[t])
    for k in range(len(column)):
        part = functools.reduce(jnp.maximum, [masked[t][k] for t in range(len(left))])
        part_ref[pl.ds(k, 1), :] = jnp.max(part, axis=0, keepdims=True)


def cost(lefts, column):
    cells = column[0].size
    return pl.CostEstimate(
        flops=2 * LANES * lefts * len(column) * cells,
        bytes_accessed=2 * cells * (lefts + len(column)),
        transcendentals=0,
    )


def column_order(count):
    return [0, 2, 1, 3] if count == 4 else list(range(count))


def on_device(embeds, assignment):
    rows = embeds.shape[0]
    columns, lanes = lax.axis_size("dev"), lax.axis_size("sub")
    order = column_order(columns)

    def along_dev(value, step):
        pairs = [(order[i], order[(i + step) % columns]) for i in range(columns)]
        return lax.ppermute(value, "dev", pairs)

    def along_sub(value, flip):
        return lax.ppermute(value, "sub", [(i, i ^ flip) for i in range(lanes)])

    own = pack(embeds, assignment)
    turns = list(range(1, (columns + 1) // 2))
    left = [along_dev(own, step) for step in turns]
    if columns % 2 == 0:
        left.append(along_dev(own, columns // 2))
    column = [own] + [along_sub(own, flip) for flip in range(1, lanes)]

    named = [(("left", t), value) for t, value in enumerate(left)]
    named += [(("column", k), value) for k, value in enumerate(column)]
    first = [('left', 0), ('column', 2), ('left', 1), ('column', 3), ('column', 1)]
    named.sort(key=lambda item: -first.index(item[0]) if item[0] in first else 1)
    blocks = [value for _, value in named]
    names = [name for name, _ in named]
    place = {
        "left": [names.index(("left", t)) for t in range(len(left))],
        "column": [names.index(("column", k)) for k in range(lanes)],
    }
    turn_best, part = pl.pallas_call(
        functools.partial(moved_kernel, rows=rows, place=place),
        out_shape=[
            jax.ShapeDtypeStruct((len(turns), 1, rows), jnp.float32),
            jax.ShapeDtypeStruct((lanes, rows), jnp.float32),
        ],
        cost_estimate=cost(len(left), column),
        compiler_params=pltpu.CompilerParams(vmem_limit_bytes=VMEM_BYTES),
    )(*blocks)
    own_best = pl.pallas_call(
        functools.partial(own_kernel, rows=rows, place=place),
        out_shape=jax.ShapeDtypeStruct((1, rows), jnp.float32),
        cost_estimate=cost(1, column),
        compiler_params=pltpu.CompilerParams(vmem_limit_bytes=VMEM_BYTES),
    )(*blocks)

    best = [own_best] + [along_dev(turn_best[t], -step) for t, step in enumerate(turns)]
    pair = part[:2]
    for flip in range(2, lanes, 2):
        pair = jnp.maximum(pair, along_sub(part[flip : flip + 2], flip))
    best.append(pair[:1])
    best.append(along_sub(pair[1:], 1))
    return functools.reduce(jnp.maximum, best).reshape(rows)


def solution(mesh):
    placed = (P(("groups", "dev", "sub"), None), P(("groups", "dev", "sub")))
    return jax.shard_map(
        on_device,
        mesh=mesh,
        in_specs=placed,
        out_specs=P(("groups", "dev", "sub")),
        check_vma=False,
    )
```

```python
import functools

import jax
import jax.numpy as jnp
from jax import lax
from jax.experimental import pallas as pl
from jax.experimental.pallas import tpu as pltpu
from jax.sharding import PartitionSpec as P

LANES = 128
ID_ROWS = 16
LOWEST = -1.0
CHUNKS = 1
VMEM_BYTES = 16 * 1024 * 1024


def pack_kernel(embeds_hbm, ids_hbm, out_ref, embeds_ref, ids_ref, embeds_sems, ids_sem):
    rows, width = embeds_ref.shape
    some = rows // CHUNKS
    copies = [
        pltpu.make_async_copy(
            embeds_hbm.at[pl.ds(c * some, some), :],
            embeds_ref.at[pl.ds(c * some, some), :],
            embeds_sems.at[c],
        )
        for c in range(CHUNKS)
    ]
    copy_ids = pltpu.make_async_copy(ids_hbm, ids_ref, ids_sem)
    copy_ids.start()
    for copy in copies:
        copy.start()
    copy_ids.wait()
    ids = ids_ref[...].astype(jnp.float32)
    out_ref[pl.ds(width // LANES * rows, ID_ROWS), :] = jnp.broadcast_to(
        ids, (ID_ROWS, rows)
    ).astype(jnp.bfloat16)
    for c, copy in enumerate(copies):
        copy.wait()
        embeds = embeds_ref[pl.ds(c * some, some), :]
        squares = jnp.sum(embeds * embeds, axis=1, keepdims=True)
        unit = (embeds * lax.rsqrt(squares + 1e-06)).astype(jnp.bfloat16)
        for block in range(width // LANES):
            out_ref[pl.ds(block * rows + c * some, some), :] = unit[
                :, block * LANES : (block + 1) * LANES
            ]


def pack(embeds, ids):
    rows, width = embeds.shape
    operands = [
        pltpu.with_memory_space_constraint(value, pltpu.HBM)
        for value in (embeds, ids.reshape(1, rows))
    ]
    return pl.pallas_call(
        pack_kernel,
        out_shape=jax.ShapeDtypeStruct((width // LANES * rows + ID_ROWS, LANES), jnp.bfloat16),
        in_specs=[pl.BlockSpec(memory_space=pltpu.HBM)] * 2,
        scratch_shapes=[
            pltpu.VMEM((rows, width), jnp.float32),
            pltpu.VMEM((1, rows), jnp.int32),
            pltpu.SemaphoreType.DMA((CHUNKS,)),
            pltpu.SemaphoreType.DMA,
        ],
        compiler_params=pltpu.CompilerParams(vmem_limit_bytes=VMEM_BYTES),
    )(*operands)


def load_rows(ref, rows):
    blocks = (ref.shape[0] - ID_ROWS) // rows
    return jnp.concatenate([ref[pl.ds(b * rows, rows), :] for b in range(blocks)], axis=1)


def load_ids(ref):
    start = ref.shape[0] - ID_ROWS
    return ref[pl.ds(start, ID_ROWS), :].astype(jnp.float32)[:1, :]


def masked_scores(left_refs, column_refs, rows, own):
    left = jnp.concatenate([load_rows(ref, rows) for ref in left_refs], axis=0)
    left_ids = [jnp.broadcast_to(load_ids(ref), (rows, rows)).T for ref in left_refs]
    masked = [[] for _ in left_refs]
    for start in range(0, len(column_refs), 4):
        refs = column_refs[start : start + 4]
        scores = lax.dot_general(
            left,
            jnp.concatenate([load_rows(ref, rows) for ref in refs], axis=0),
            (((1,), (1,)), ((), ())),
            preferred_element_type=jnp.float32,
        )
        for j, ref in enumerate(refs):
            ids = load_ids(ref)
            for t in range(len(left_refs)):
                same = left_ids[t] == ids
                if own and start + j == 0:
                    down = lax.broadcasted_iota(jnp.int32, (rows, rows), 0)
                    across = lax.broadcasted_iota(jnp.int32, (rows, rows), 1)
                    same = same & (down != across)
                part = scores[t * rows : (t + 1) * rows, j * rows : (j + 1) * rows]
                masked[t].append(jnp.where(same, part, jnp.float32(LOWEST)))
    return masked


def row_maxima(masked):
    best = functools.reduce(jnp.maximum, masked)
    return jnp.max(best.T, axis=0, keepdims=True)


def own_kernel(*refs, rows, place):
    column = [refs[i] for i in place["column"]]
    refs[-1][...] = row_maxima(masked_scores(column[:1], column, rows, True)[0])


def moved_kernel(*refs, rows, place):
    left = [refs[i] for i in place["left"]]
    column = [refs[i] for i in place["column"]]
    turn_ref, part_ref = refs[-2:]
    masked = masked_scores(left, column, rows, False)
    for t in range(turn_ref.shape[0]):
        turn_ref[t] = row_maxima(masked[t])
    for k in range(len(column)):
        part = functools.reduce(jnp.maximum, [masked[t][k] for t in range(len(left))])
        part_ref[pl.ds(k, 1), :] = jnp.max(part, axis=0, keepdims=True)


def cost(lefts, column):
    cells = column[0].size
    return pl.CostEstimate(
        flops=2 * LANES * lefts * len(column) * cells,
        bytes_accessed=2 * cells * (lefts + len(column)),
        transcendentals=0,
    )


def column_order(count):
    return [0, 2, 1, 3] if count == 4 else list(range(count))


def on_device(embeds, assignment):
    rows = embeds.shape[0]
    columns, lanes = lax.axis_size("dev"), lax.axis_size("sub")
    order = column_order(columns)

    def along_dev(value, step):
        pairs = [(order[i], order[(i + step) % columns]) for i in range(columns)]
        return lax.ppermute(value, "dev", pairs)

    def along_sub(value, flip):
        return lax.ppermute(value, "sub", [(i, i ^ flip) for i in range(lanes)])

    own = pack(embeds, assignment)
    turns = list(range(1, (columns + 1) // 2))
    left = [along_dev(own, step) for step in turns]
    if columns % 2 == 0:
        left.append(along_dev(own, columns // 2))
    column = [own] + [along_sub(own, flip) for flip in range(1, lanes)]

    named = [(("left", t), value) for t, value in enumerate(left)]
    named += [(("column", k), value) for k, value in enumerate(column)]
    first = [('left', 0), ('column', 2), ('left', 1), ('column', 3), ('column', 1)]
    named.sort(key=lambda item: -first.index(item[0]) if item[0] in first else 1)
    blocks = [value for _, value in named]
    names = [name for name, _ in named]
    place = {
        "left": [names.index(("left", t)) for t in range(len(left))],
        "column": [names.index(("column", k)) for k in range(lanes)],
    }
    turn_best, part = pl.pallas_call(
        functools.partial(moved_kernel, rows=rows, place=place),
        out_shape=[
            jax.ShapeDtypeStruct((len(turns), 1, rows), jnp.float32),
            jax.ShapeDtypeStruct((lanes, rows), jnp.float32),
        ],
        cost_estimate=cost(len(left), column),
        compiler_params=pltpu.CompilerParams(vmem_limit_bytes=VMEM_BYTES),
    )(*blocks)
    own_best = pl.pallas_call(
        functools.partial(own_kernel, rows=rows, place=place),
        out_shape=jax.ShapeDtypeStruct((1, rows), jnp.float32),
        cost_estimate=cost(1, column),
        compiler_params=pltpu.CompilerParams(vmem_limit_bytes=VMEM_BYTES),
    )(*blocks)

    best = [own_best] + [along_dev(turn_best[t], -step) for t, step in enumerate(turns)]
    pair = part[:2]
    for flip in range(2, lanes, 2):
        pair = jnp.maximum(pair, along_sub(part[flip : flip + 2], flip))
    best.append(pair[:1])
    best.append(along_sub(pair[1:], 1))
    return functools.reduce(jnp.maximum, best).reshape(rows)


def solution(mesh):
    placed = (P(("groups", "dev", "sub"), None), P(("groups", "dev", "sub")))
    return jax.shard_map(
        on_device,
        mesh=mesh,
        in_specs=placed,
        out_specs=P(("groups", "dev", "sub")),
        check_vma=False,
    )
```

```python
import functools

import jax
import jax.numpy as jnp
from jax import lax
from jax.experimental import pallas as pl
from jax.experimental.pallas import tpu as pltpu
from jax.sharding import PartitionSpec as P

LANES = 128
ID_ROWS = 16
LOWEST = -1.0
CHUNKS = 1
VMEM_BYTES = 16 * 1024 * 1024


def pack_kernel(embeds_hbm, ids_hbm, out_ref, embeds_ref, ids_ref, embeds_sems, ids_sem):
    rows, width = embeds_ref.shape
    some = rows // CHUNKS
    copies = [
        pltpu.make_async_copy(
            embeds_hbm.at[pl.ds(c * some, some), :],
            embeds_ref.at[pl.ds(c * some, some), :],
            embeds_sems.at[c],
        )
        for c in range(CHUNKS)
    ]
    copy_ids = pltpu.make_async_copy(ids_hbm, ids_ref, ids_sem)
    copy_ids.start()
    for copy in copies:
        copy.start()
    copy_ids.wait()
    ids = ids_ref[...].astype(jnp.float32)
    out_ref[pl.ds(width // LANES * rows, ID_ROWS), :] = jnp.broadcast_to(
        ids, (ID_ROWS, rows)
    ).astype(jnp.bfloat16)
    for c, copy in enumerate(copies):
        copy.wait()
        embeds = embeds_ref[pl.ds(c * some, some), :]
        squares = jnp.sum(embeds * embeds, axis=1, keepdims=True)
        unit = (embeds * lax.rsqrt(squares + 1e-06)).astype(jnp.bfloat16)
        for block in range(width // LANES):
            out_ref[pl.ds(block * rows + c * some, some), :] = unit[
                :, block * LANES : (block + 1) * LANES
            ]


def pack(embeds, ids):
    rows, width = embeds.shape
    operands = [
        pltpu.with_memory_space_constraint(value, pltpu.HBM)
        for value in (embeds, ids.reshape(1, rows))
    ]
    return pl.pallas_call(
        pack_kernel,
        out_shape=jax.ShapeDtypeStruct((width // LANES * rows + ID_ROWS, LANES), jnp.bfloat16),
        in_specs=[pl.BlockSpec(memory_space=pltpu.HBM)] * 2,
        scratch_shapes=[
            pltpu.VMEM((rows, width), jnp.float32),
            pltpu.VMEM((1, rows), jnp.int32),
            pltpu.SemaphoreType.DMA((CHUNKS,)),
            pltpu.SemaphoreType.DMA,
        ],
        compiler_params=pltpu.CompilerParams(vmem_limit_bytes=VMEM_BYTES),
    )(*operands)


def load_rows(ref, rows):
    blocks = (ref.shape[0] - ID_ROWS) // rows
    return jnp.concatenate([ref[pl.ds(b * rows, rows), :] for b in range(blocks)], axis=1)


def load_ids(ref):
    start = ref.shape[0] - ID_ROWS
    return ref[pl.ds(start, ID_ROWS), :].astype(jnp.float32)[:1, :]


def masked_scores(left_refs, column_refs, rows, own):
    left = jnp.concatenate([load_rows(ref, rows) for ref in left_refs], axis=0)
    left_ids = [jnp.broadcast_to(load_ids(ref), (rows, rows)).T for ref in left_refs]
    masked = [[] for _ in left_refs]
    for start in range(0, len(column_refs), 4):
        refs = column_refs[start : start + 4]
        scores = lax.dot_general(
            left,
            jnp.concatenate([load_rows(ref, rows) for ref in refs], axis=0),
            (((1,), (1,)), ((), ())),
            preferred_element_type=jnp.float32,
        )
        for j, ref in enumerate(refs):
            ids = load_ids(ref)
            for t in range(len(left_refs)):
                same = left_ids[t] == ids
                if own and start + j == 0:
                    down = lax.broadcasted_iota(jnp.int32, (rows, rows), 0)
                    across = lax.broadcasted_iota(jnp.int32, (rows, rows), 1)
                    same = same & (down != across)
                part = scores[t * rows : (t + 1) * rows, j * rows : (j + 1) * rows]
                masked[t].append(jnp.where(same, part, jnp.float32(LOWEST)))
    return masked


def row_maxima(masked):
    best = functools.reduce(jnp.maximum, masked)
    return jnp.max(best.T, axis=0, keepdims=True)


def own_kernel(*refs, rows, place):
    column = [refs[i] for i in place["column"]]
    refs[-1][...] = row_maxima(masked_scores(column[:1], column, rows, True)[0])


def moved_kernel(*refs, rows, place, last):
    left = [refs[i] for i in place["left"]]
    column = [refs[i] for i in place["column"]]
    turn_ref, part_ref = refs[-2:]
    masked = masked_scores(left, column, rows, False)
    for t in range(len(left)):
        turn_ref[t] = row_maxima(masked[t])
    parts = []
    for k in range(len(column)):
        part = functools.reduce(jnp.maximum, [masked[t][k] for t in range(len(left))])
        parts.append(jnp.max(part, axis=0, keepdims=True))
    if last:
        here = lax.axis_index("dev") == last
        parts[1], parts[2] = (
            jnp.where(here, parts[2], parts[1]),
            jnp.where(here, parts[1], parts[2]),
        )
    for k, part in enumerate(parts):
        part_ref[pl.ds(k, 1), :] = part


def cost(lefts, column):
    cells = column[0].size
    return pl.CostEstimate(
        flops=2 * LANES * lefts * len(column) * cells,
        bytes_accessed=2 * cells * (lefts + len(column)),
        transcendentals=0,
    )


def column_order(count):
    return [0, 2, 1, 3] if count == 4 else list(range(count))


def on_device(embeds, assignment):
    rows = embeds.shape[0]
    columns, lanes = lax.axis_size("dev"), lax.axis_size("sub")
    order = column_order(columns)

    def along_dev(value, steps):
        pairs = [
            (order[i] * lanes + k, order[(i + steps[k % 2]) % columns] * lanes + k)
            for i in range(columns)
            for k in range(lanes)
        ]
        return lax.ppermute(value, ("dev", "sub"), pairs)

    def along_sub(value, flip):
        return lax.ppermute(value, "sub", [(i, i ^ flip) for i in range(lanes)])

    last = columns - 1 if lanes == 4 else 0

    def by_column(value, flip, last_flip):
        pairs = [
            (i * lanes + k, i * lanes + (k ^ (last_flip if i == last else flip)))
            for i in range(columns)
            for k in range(lanes)
        ]
        return lax.ppermute(value, ("dev", "sub"), pairs)

    own = pack(embeds, assignment)
    steps = list(range(1, columns // 2 + 1))
    turns = steps[: (columns - 1) // 2]
    left = [along_dev(own, pair) for pair in zip(steps, steps[::-1])]
    column = [own] + [along_sub(own, flip) for flip in range(1, lanes)]

    named = [(("left", t), value) for t, value in enumerate(left)]
    named += [(("column", k), value) for k, value in enumerate(column)]
    first = [('left', 0), ('column', 2), ('column', 3), ('left', 1), ('column', 1)]
    named.sort(key=lambda item: -first.index(item[0]) if item[0] in first else 1)
    blocks = [value for _, value in named]
    names = [name for name, _ in named]
    place = {
        "left": [names.index(("left", t)) for t in range(len(left))],
        "column": [names.index(("column", k)) for k in range(lanes)],
    }
    turn_best, part = pl.pallas_call(
        functools.partial(moved_kernel, rows=rows, place=place, last=last),
        out_shape=[
            jax.ShapeDtypeStruct((len(left), 1, rows), jnp.float32),
            jax.ShapeDtypeStruct((lanes, rows), jnp.float32),
        ],
        cost_estimate=cost(len(left), column),
        compiler_params=pltpu.CompilerParams(vmem_limit_bytes=VMEM_BYTES),
    )(*blocks)
    own_best = pl.pallas_call(
        functools.partial(own_kernel, rows=rows, place=place),
        out_shape=jax.ShapeDtypeStruct((1, rows), jnp.float32),
        cost_estimate=cost(1, column),
        compiler_params=pltpu.CompilerParams(vmem_limit_bytes=VMEM_BYTES),
    )(*blocks)

    odd = lax.axis_index("sub") % 2 == 1
    best = [own_best]
    for t, step in enumerate(turns):
        back = jnp.where(odd, turn_best[len(steps) - 1 - t], turn_best[t])
        best.append(along_dev(back, (-step, -step)))
    if last:
        pair = jnp.maximum(part[:2], by_column(part[2:], 2, 1))
        best.append(by_column(pair[1:], 1, 2))
    else:
        pair = part[:2]
        for flip in range(2, lanes, 2):
            pair = jnp.maximum(pair, along_sub(part[flip : flip + 2], flip))
        best.append(along_sub(pair[1:], 1))
    best.append(pair[:1])
    return functools.reduce(jnp.maximum, best).reshape(rows)


def solution(mesh):
    placed = (P(("groups", "dev", "sub"), None), P(("groups", "dev", "sub")))
    return jax.shard_map(
        on_device,
        mesh=mesh,
        in_specs=placed,
        out_specs=P(("groups", "dev", "sub")),
        check_vma=False,
    )
```

```python
import functools

import jax
import jax.numpy as jnp
from jax import lax
from jax.experimental import pallas as pl
from jax.experimental.pallas import tpu as pltpu
from jax.sharding import PartitionSpec as P

LANES = 128
ID_ROWS = 16
LOWEST = -1.0
ORDERS = (('turn', 'x', 'swap'), ('x', 'swap', 'turn'))
CHUNKS = 1
VMEM_BYTES = 16 * 1024 * 1024


def pack_kernel(embeds_hbm, ids_hbm, out_ref, embeds_ref, ids_ref, embeds_sems, ids_sem):
    rows, width = embeds_ref.shape
    some = rows // CHUNKS
    copies = [
        pltpu.make_async_copy(
            embeds_hbm.at[pl.ds(c * some, some), :],
            embeds_ref.at[pl.ds(c * some, some), :],
            embeds_sems.at[c],
        )
        for c in range(CHUNKS)
    ]
    copy_ids = pltpu.make_async_copy(ids_hbm, ids_ref, ids_sem)
    for copy in copies:
        copy.start()
    copy_ids.start()
    copy_ids.wait()
    ids = ids_ref[...].astype(jnp.float32)
    out_ref[pl.ds(width // LANES * rows, ID_ROWS), :] = jnp.broadcast_to(
        ids, (ID_ROWS, rows)
    ).astype(jnp.bfloat16)
    for c, copy in enumerate(copies):
        copy.wait()
        embeds = embeds_ref[pl.ds(c * some, some), :]
        squares = jnp.sum(embeds * embeds, axis=1, keepdims=True)
        unit = (embeds * lax.rsqrt(squares + 1e-06)).astype(jnp.bfloat16)
        for block in range(width // LANES):
            out_ref[pl.ds(block * rows + c * some, some), :] = unit[
                :, block * LANES : (block + 1) * LANES
            ]


def pack(embeds, ids):
    rows, width = embeds.shape
    operands = [
        pltpu.with_memory_space_constraint(value, pltpu.HBM)
        for value in (embeds, ids.reshape(1, rows))
    ]
    return pl.pallas_call(
        pack_kernel,
        out_shape=jax.ShapeDtypeStruct((width // LANES * rows + ID_ROWS, LANES), jnp.bfloat16),
        in_specs=[pl.BlockSpec(memory_space=pltpu.HBM)] * 2,
        scratch_shapes=[
            pltpu.VMEM((rows, width), jnp.float32),
            pltpu.VMEM((1, rows), jnp.int32),
            pltpu.SemaphoreType.DMA((CHUNKS,)),
            pltpu.SemaphoreType.DMA,
        ],
        compiler_params=pltpu.CompilerParams(vmem_limit_bytes=VMEM_BYTES),
    )(*operands)


def load(ref):
    start = ref.shape[0] - ID_ROWS
    parts = [ref[pl.ds(b * LANES, LANES), :] for b in range(start // LANES)]
    return jnp.concatenate(parts, axis=1), ref[pl.ds(start, ID_ROWS), :]


def choose(here, one, other):
    return jax.tree.map(lambda a, b: jnp.where(here, a, b), one, other)


def masked_scores(left, column, rows, own):
    line = [ids.astype(jnp.float32)[:1, :] for _, ids in column]
    scores = lax.dot_general(
        jnp.concatenate([value for value, _ in left], axis=0),
        jnp.concatenate([value for value, _ in column], axis=0),
        (((1,), (1,)), ((), ())),
        preferred_element_type=jnp.float32,
    )
    masked = []
    for t, (_, ids) in enumerate(left):
        left_ids = jnp.broadcast_to(ids.astype(jnp.float32)[:1, :], (rows, rows)).T
        masked.append([])
        for k in range(len(column)):
            same = left_ids == line[k]
            if own and k == 0:
                down = lax.broadcasted_iota(jnp.int32, (rows, rows), 0)
                across = lax.broadcasted_iota(jnp.int32, (rows, rows), 1)
                same = same & (down != across)
            part = scores[t * rows : (t + 1) * rows, k * rows : (k + 1) * rows]
            masked[t].append(jnp.where(same, part, jnp.float32(LOWEST)))
    return masked


def row_maxima(masked):
    best = functools.reduce(jnp.maximum, masked)
    return jnp.max(best.T, axis=0, keepdims=True)


def unpack(refs, place):
    left = [load(refs[i]) for i in place["left"]]
    column = [load(refs[i]) for i in place["column"]]
    if len(left) == 3:
        odd = lax.rem(lax.axis_index("sub"), 2) == 1
        even_x, odd_x = (moves.index("x") for moves in ORDERS)
        column.insert(2, choose(odd, left[odd_x], left[even_x]))
        if even_x != odd_x:
            left[even_x] = choose(odd, left[even_x], left[odd_x])
        del left[odd_x]
    return left, column


def own_kernel(*refs, rows, place):
    _, column = unpack(refs[:-1], place)
    refs[-1][...] = row_maxima(masked_scores(column[:1], column, rows, True)[0])


def rotation_places():
    even_x, odd_x = (moves.index("x") for moves in ORDERS)
    even = [move for i, move in enumerate(ORDERS[0])]
    odd = [move for i, move in enumerate(ORDERS[1])]
    if even_x != odd_x:
        even[even_x] = even[odd_x]
        odd[even_x] = odd[even_x]
    del even[odd_x], odd[odd_x]
    return even.index("turn"), odd.index("turn")


def moved_kernel(*refs, rows, place, turns, last):
    left, column = unpack(refs, place)
    *turn_refs, pass_ref, keep_ref = refs[-2 - max(turns, 1) :]
    masked = masked_scores(left, column, rows, False)
    odd = lax.rem(lax.axis_index("sub"), 2) == 1
    for t in range(turns):
        best = functools.reduce(jnp.maximum, masked[t])
        if last:
            even_turn, odd_turn = rotation_places()
            best = functools.reduce(jnp.maximum, masked[even_turn])
            other = functools.reduce(jnp.maximum, masked[odd_turn])
            best = jnp.where(odd, other, best)
        elif len(left) > 1:
            other = functools.reduce(jnp.maximum, masked[-1 - t])
            best = jnp.where(odd, other, best)
        turn_refs[t][...] = jnp.max(best.T, axis=0, keepdims=True)
    parts = []
    for k in range(len(column)):
        part = functools.reduce(jnp.maximum, [masked[t][k] for t in range(len(left))])
        parts.append(jnp.max(part, axis=0, keepdims=True))
    if last:
        here = lax.axis_index("dev") == last
        parts[1], parts[2] = (
            jnp.where(here, parts[2], parts[1]),
            jnp.where(here, parts[1], parts[2]),
        )
    for k, part in enumerate(parts):
        ref, row = (keep_ref, k) if k < 2 else (pass_ref, k - 2)
        ref[pl.ds(row, 1), :] = part


def cost(lefts, column):
    cells = column[0].size
    return pl.CostEstimate(
        flops=2 * LANES * lefts * len(column) * cells,
        bytes_accessed=2 * cells * (lefts + len(column)),
        transcendentals=0,
    )


def column_order(count):
    return [0, 2, 1, 3] if count == 4 else list(range(count))


def on_device(embeds, assignment):
    rows = embeds.shape[0]
    columns, lanes = lax.axis_size("dev"), lax.axis_size("sub")
    order = column_order(columns)

    def along_dev(value, steps):
        pairs = [
            (order[i] * lanes + k, order[(i + steps[k % 2]) % columns] * lanes + k)
            for i in range(columns)
            for k in range(lanes)
        ]
        return lax.ppermute(value, ("dev", "sub"), pairs)

    def along_sub(value, flip):
        return lax.ppermute(value, "sub", [(i, i ^ flip) for i in range(lanes)])

    last = columns - 1 if lanes == 4 and columns == 4 else 0

    def by_column(value, flip, last_flip):
        pairs = [
            (i * lanes + k, i * lanes + (k ^ (last_flip if i == last else flip)))
            for i in range(columns)
            for k in range(lanes)
        ]
        return lax.ppermute(value, ("dev", "sub"), pairs)

    own = pack(embeds, assignment)
    steps = list(range(1, columns // 2 + 1))
    turns = steps[: (columns - 1) // 2]
    if last:
        left = []
        for moves in zip(*ORDERS):
            pairs = []
            for i in range(columns):
                for k in range(lanes):
                    move = moves[k % 2]
                    step = {"turn": 1, "swap": 2, "x": 0}[move]
                    j = order[(order.index(i) + step) % columns]
                    pairs.append((i * lanes + k, j * lanes + (k ^ 2 if move == "x" else k)))
            left.append(lax.ppermute(own, ("dev", "sub"), pairs))
        column = [own, along_sub(own, 1), along_sub(own, 3)]
    else:
        left = [along_dev(own, pair) for pair in zip(steps, steps[::-1])]
        column = [own] + [along_sub(own, flip) for flip in range(1, lanes)]

    named = [(("left", t), value) for t, value in enumerate(left)]
    named += [(("column", k), value) for k, value in enumerate(column)]
    first = [('left', 0), ('left', 1), ('column', 1), ('left', 2), ('column', 2)]
    named.sort(key=lambda item: -first.index(item[0]) if item[0] in first else 1)
    blocks = [value for _, value in named]
    names = [name for name, _ in named]
    place = {
        "left": [names.index(("left", t)) for t in range(len(left))],
        "column": [names.index(("column", k)) for k in range(len(column))],
    }
    line = jax.ShapeDtypeStruct((1, rows), jnp.float32)
    *back, passed, kept = pl.pallas_call(
        functools.partial(moved_kernel, rows=rows, place=place, turns=len(turns), last=last),
        out_shape=[line] * max(len(turns), 1)
        + [
            jax.ShapeDtypeStruct((max(lanes - 2, 1), rows), jnp.float32),
            jax.ShapeDtypeStruct((2, rows), jnp.float32),
        ],
        cost_estimate=cost(2, column),
        compiler_params=pltpu.CompilerParams(vmem_limit_bytes=VMEM_BYTES),
    )(*blocks)
    own_best = pl.pallas_call(
        functools.partial(own_kernel, rows=rows, place=place),
        out_shape=jax.ShapeDtypeStruct((1, rows), jnp.float32),
        cost_estimate=cost(1, column),
        compiler_params=pltpu.CompilerParams(vmem_limit_bytes=VMEM_BYTES),
    )(*blocks)

    best = [own_best]
    for value, step in zip(back, turns):
        best.append(along_dev(value, (-step, -step)))
    if last:
        pair = jnp.maximum(kept, by_column(passed, 2, 1))
        best.append(by_column(pair[1:], 1, 2))
    else:
        pair = kept
        for flip in range(2, lanes, 2):
            pair = jnp.maximum(pair, along_sub(passed[flip - 2 : flip], flip))
        best.append(along_sub(pair[1:], 1))
    best.append(pair[:1])
    return functools.reduce(jnp.maximum, best).reshape(rows)


def solution(mesh):
    placed = (P(("groups", "dev", "sub"), None), P(("groups", "dev", "sub")))
    return jax.shard_map(
        on_device,
        mesh=mesh,
        in_specs=placed,
        out_specs=P(("groups", "dev", "sub")),
        check_vma=False,
    )
```

```python
import functools

import jax
import jax.numpy as jnp
from jax import lax
from jax.experimental import pallas as pl
from jax.experimental.pallas import tpu as pltpu
from jax.sharding import PartitionSpec as P

LANES = 128
ID_ROWS = 16
LOWEST = -1.0
CHUNKS = 1
VMEM_BYTES = 16 * 1024 * 1024


def pack_kernel(embeds_hbm, ids_hbm, out_ref, embeds_ref, ids_ref, embeds_sems, ids_sem):
    rows, width = embeds_ref.shape
    some = rows // CHUNKS
    copies = [
        pltpu.make_async_copy(
            embeds_hbm.at[pl.ds(c * some, some), :],
            embeds_ref.at[pl.ds(c * some, some), :],
            embeds_sems.at[c],
        )
        for c in range(CHUNKS)
    ]
    copy_ids = pltpu.make_async_copy(ids_hbm, ids_ref, ids_sem)
    for copy in copies:
        copy.start()
    copy_ids.start()
    copy_ids.wait()
    ids = ids_ref[...].astype(jnp.float32)
    out_ref[pl.ds(width // LANES * rows, ID_ROWS), :] = jnp.broadcast_to(
        ids, (ID_ROWS, rows)
    ).astype(jnp.bfloat16)
    for c, copy in enumerate(copies):
        copy.wait()
        embeds = embeds_ref[pl.ds(c * some, some), :]
        squares = jnp.sum(embeds * embeds, axis=1, keepdims=True)
        unit = (embeds * lax.rsqrt(squares + 1e-06)).astype(jnp.bfloat16)
        for block in range(width // LANES):
            out_ref[pl.ds(block * rows + c * some, some), :] = unit[
                :, block * LANES : (block + 1) * LANES
            ]


def pack(embeds, ids):
    rows, width = embeds.shape
    operands = [
        pltpu.with_memory_space_constraint(value, pltpu.HBM)
        for value in (embeds, ids.reshape(1, rows))
    ]
    return pl.pallas_call(
        pack_kernel,
        out_shape=jax.ShapeDtypeStruct((width // LANES * rows + ID_ROWS, LANES), jnp.bfloat16),
        in_specs=[pl.BlockSpec(memory_space=pltpu.HBM)] * 2,
        scratch_shapes=[
            pltpu.VMEM((rows, width), jnp.float32),
            pltpu.VMEM((1, rows), jnp.int32),
            pltpu.SemaphoreType.DMA((CHUNKS,)),
            pltpu.SemaphoreType.DMA,
        ],
        compiler_params=pltpu.CompilerParams(vmem_limit_bytes=VMEM_BYTES),
    )(*operands)


def load_rows(ref, rows):
    blocks = (ref.shape[0] - ID_ROWS) // rows
    return jnp.concatenate([ref[pl.ds(b * rows, rows), :] for b in range(blocks)], axis=1)


def load_ids(ref):
    start = ref.shape[0] - ID_ROWS
    return ref[pl.ds(start, ID_ROWS), :].astype(jnp.float32)[:1, :]


def masked_scores(left_refs, column_refs, rows, own):
    left = jnp.concatenate([load_rows(ref, rows) for ref in left_refs], axis=0)
    left_ids = [jnp.broadcast_to(load_ids(ref), (rows, rows)).T for ref in left_refs]
    masked = [[] for _ in left_refs]
    for start in range(0, len(column_refs), 4):
        refs = column_refs[start : start + 4]
        scores = lax.dot_general(
            left,
            jnp.concatenate([load_rows(ref, rows) for ref in refs], axis=0),
            (((1,), (1,)), ((), ())),
            preferred_element_type=jnp.float32,
        )
        for j, ref in enumerate(refs):
            ids = load_ids(ref)
            for t in range(len(left_refs)):
                same = left_ids[t] == ids
                if own and start + j == 0:
                    down = lax.broadcasted_iota(jnp.int32, (rows, rows), 0)
                    across = lax.broadcasted_iota(jnp.int32, (rows, rows), 1)
                    same = same & (down != across)
                part = scores[t * rows : (t + 1) * rows, j * rows : (j + 1) * rows]
                masked[t].append(jnp.where(same, part, jnp.float32(LOWEST)))
    return masked


def row_maxima(masked):
    best = functools.reduce(jnp.maximum, masked)
    return jnp.max(best.T, axis=0, keepdims=True)


def own_kernel(*refs, rows, place):
    column = [refs[i] for i in place["column"]]
    refs[-1][...] = row_maxima(masked_scores(column[:1], column, rows, True)[0])


def moved_kernel(*refs, rows, place, turns, last):
    left = [refs[i] for i in place["left"]]
    column = [refs[i] for i in place["column"]]
    *turn_refs, pass_ref, keep_ref = refs[-2 - max(turns, 1) :]
    masked = masked_scores(left, column, rows, False)
    odd = lax.rem(lax.axis_index("sub"), 2) == 1
    for t in range(turns):
        best = functools.reduce(jnp.maximum, masked[t])
        if len(left) > 1:
            other = functools.reduce(jnp.maximum, masked[-1 - t])
            best = jnp.where(odd, other, best)
        turn_refs[t][...] = jnp.max(best.T, axis=0, keepdims=True)
    parts = []
    for k in range(len(column)):
        part = functools.reduce(jnp.maximum, [masked[t][k] for t in range(len(left))])
        parts.append(jnp.max(part, axis=0, keepdims=True))
    if last:
        here = lax.axis_index("dev") == last
        parts[1], parts[2] = (
            jnp.where(here, parts[2], parts[1]),
            jnp.where(here, parts[1], parts[2]),
        )
    for k, part in enumerate(parts):
        ref, row = (keep_ref, k) if k < 2 else (pass_ref, k - 2)
        ref[pl.ds(row, 1), :] = part


def cost(lefts, column):
    cells = column[0].size
    return pl.CostEstimate(
        flops=2 * LANES * lefts * len(column) * cells,
        bytes_accessed=2 * cells * (lefts + len(column)),
        transcendentals=0,
    )


def column_order(count):
    return [0, 2, 1, 3] if count == 4 else list(range(count))


def on_device(embeds, assignment):
    rows = embeds.shape[0]
    columns, lanes = lax.axis_size("dev"), lax.axis_size("sub")
    order = column_order(columns)

    def along_dev(value, steps):
        pairs = [
            (order[i] * lanes + k, order[(i + steps[k % 2]) % columns] * lanes + k)
            for i in range(columns)
            for k in range(lanes)
        ]
        return lax.ppermute(value, ("dev", "sub"), pairs)

    def along_sub(value, flip):
        return lax.ppermute(value, "sub", [(i, i ^ flip) for i in range(lanes)])

    last = columns - 1 if lanes == 4 else 0

    def by_column(value, flip, last_flip):
        pairs = [
            (i * lanes + k, i * lanes + (k ^ (last_flip if i == last else flip)))
            for i in range(columns)
            for k in range(lanes)
        ]
        return lax.ppermute(value, ("dev", "sub"), pairs)

    own = pack(embeds, assignment)
    steps = list(range(1, columns // 2 + 1))
    turns = steps[: (columns - 1) // 2]
    left = [along_dev(own, pair) for pair in zip(steps, steps[::-1])]
    column = [own] + [along_sub(own, flip) for flip in range(1, lanes)]

    named = [(("left", t), value) for t, value in enumerate(left)]
    named += [(("column", k), value) for k, value in enumerate(column)]
    first = [('left', 0), ('column', 2), ('column', 3), ('left', 1), ('column', 1)]
    named.sort(key=lambda item: -first.index(item[0]) if item[0] in first else 1)
    blocks = [value for _, value in named]
    names = [name for name, _ in named]
    place = {
        "left": [names.index(("left", t)) for t in range(len(left))],
        "column": [names.index(("column", k)) for k in range(lanes)],
    }
    line = jax.ShapeDtypeStruct((1, rows), jnp.float32)
    *back, passed, kept = pl.pallas_call(
        functools.partial(moved_kernel, rows=rows, place=place, turns=len(turns), last=last),
        out_shape=[line] * max(len(turns), 1)
        + [
            jax.ShapeDtypeStruct((max(lanes - 2, 1), rows), jnp.float32),
            jax.ShapeDtypeStruct((2, rows), jnp.float32),
        ],
        cost_estimate=cost(len(left), column),
        compiler_params=pltpu.CompilerParams(vmem_limit_bytes=VMEM_BYTES),
    )(*blocks)
    own_best = pl.pallas_call(
        functools.partial(own_kernel, rows=rows, place=place),
        out_shape=jax.ShapeDtypeStruct((1, rows), jnp.float32),
        cost_estimate=cost(1, column),
        compiler_params=pltpu.CompilerParams(vmem_limit_bytes=VMEM_BYTES),
    )(*blocks)

    best = [own_best]
    for value, step in zip(back, turns):
        best.append(along_dev(value, (-step, -step)))
    if last:
        pair = jnp.maximum(kept, by_column(passed, 2, 1))
        best.append(by_column(pair[1:], 1, 2))
    else:
        pair = kept
        for flip in range(2, lanes, 2):
            pair = jnp.maximum(pair, along_sub(passed[flip - 2 : flip], flip))
        best.append(along_sub(pair[1:], 1))
    best.append(pair[:1])
    return functools.reduce(jnp.maximum, best).reshape(rows)


def solution(mesh):
    placed = (P(("groups", "dev", "sub"), None), P(("groups", "dev", "sub")))
    return jax.shard_map(
        on_device,
        mesh=mesh,
        in_specs=placed,
        out_specs=P(("groups", "dev", "sub")),
        check_vma=False,
    )
```
